32 devices in a mesh: grp: 2 (over x), gy: 8 (over z, y), ch: 2 (over core).
Axes of the slice: x: 2, y: 2, z: 4, core: 2. Of those that a mesh axis runs over, the one named last changes fastest.
Arguments:
- inputs: bfloat16 [256, 8, 16, 256], P(None, 'gy', 'grp'), parts along dimension 2, may hold values from -6 to 6
- cotangent: bfloat16 [256, 8, 16, 256], P('ch', 'gy', 'grp'), parts along dimension 2, may hold values from -6 to 6
- weight: bfloat16 [27, 256, 256], P(None, None, 'ch'), may hold values from -0.078125 to 0.078125
Outputs:
- input_grad: bfloat16 [256, 8, 16, 256], P('ch', 'gy', 'grp'), parts along dimension 2
- weight_grad: float32 [54, 256, 256], P('grp', None, 'ch'), parts along dimension 0
The draws below stay inside these ranges and needn't reach their ends.
There are 2 independent parts, one for each index of `grp`. The reference program is written for one: setup_inputs(seed, part) draws one part's arguments, and reference() takes and returns one part's arrays. A program takes and returns all parts, laid end to end along the dimension named above; an argument that names none is the same for every part. Nothing has to cross between parts.
All inputs are finite; a program needn't handle non-finite values.
Results may differ from the reference program's by a relative error of at most 0.0013.
Values may be sent and summed in bfloat16 or wider, within the bound.
A program may use at most 192 MiB of HBM per device.

```python
import math
import jax
import jax.numpy as jnp
from jax import lax

C = 256
X = 256
Z = 8
NY = 8


def level_of(stream_key, extent, pieces, smallest, largest):
    def one(dim, shards_of):
        heights = jax.random.uniform(jax.random.fold_in(jax.random.fold_in(stream_key, 6), dim), (shards_of,), jnp.float32, smallest / len(pieces), largest / len(pieces))
        return jnp.repeat(jnp.exp(heights), extent[dim] // shards_of).reshape((-1,) + (1,) * (len(extent) - dim - 1))

    loudness = one(*pieces[0])
    for cut in pieces[1:]:
        loudness = loudness * one(*cut)
    return loudness


def noise(own_key, dims, spread, bound, pieces=(), dtype=jnp.bfloat16):
    loudness = level_of(own_key, dims, pieces, -0.22, 0.18) if pieces else 1.0
    values = jax.random.normal(own_key, dims, jnp.float32) * spread * loudness
    return jnp.minimum(jnp.maximum(values, -bound), bound).astype(dtype)


def setup_inputs(seed: int = 0, part: int = 0) -> dict:
    seeds = jax.random.split(jax.random.key(seed), 4)
    part_keys = jax.random.split(jax.random.fold_in(seeds[3], part), 4)
    return {
        "inputs": noise(part_keys[0], (C, NY, Z, X), 1.0, 6.0, ((1, 8),)),
        "cotangent": noise(part_keys[1], (C, NY, Z, X), 1.0, 6.0, ((0, 2), (1, 8))),
        "weight": noise(seeds[2], (27, C, C), (27 * C) ** -0.5, 0.078125, ((2, 2),)),
    }


def shifted_grad(values_in, y_off, z_off, x_off):
    padded = jnp.pad(values_in, ((0, 0), (1, 1), (1, 1), (1, 1)))
    y_count = values_in.shape[1]
    z_count = values_in.shape[2]
    x_count = values_in.shape[3]
    return padded[:, 2 - y_off:2 - y_off + y_count, 2 - z_off:2 - z_off + z_count, 2 - x_off:2 - x_off + x_count]

def reference(inputs, cotangent, weight):
    channel_count = inputs.shape[0]
    inputs_flat = inputs.astype(jnp.float32).reshape(channel_count, -1)
    weight_wide = weight.astype(jnp.float32)
    grad_acc = jnp.zeros((channel_count, inputs_flat.shape[1]), jnp.float32)
    tap_grads = []
    for y_off in range(3):
        for z_off in range(3):
            for x_off in range(3):
                tap_index = 9 * y_off + 3 * z_off + x_off
                moved = shifted_grad(cotangent, y_off, z_off, x_off).astype(jnp.float32).reshape(channel_count, -1)
                grad_acc = grad_acc + jnp.dot(weight_wide[tap_index], moved, preferred_element_type=jnp.float32)
                tap_grads.append(lax.dot_general(inputs_flat, moved, (((1,), (1,)), ((), ())), preferred_element_type=jnp.float32))
    input_grad = grad_acc.astype(jnp.bfloat16).reshape(inputs.shape)
    norm_factor = 1.0 / math.sqrt(NY * Z * X)
    weight_grad = jnp.stack(tap_grads, 0) * norm_factor
    return (input_grad, weight_grad)
```

```python
import functools
import math

import jax
import jax.numpy as jnp
from jax import lax
from jax.experimental import pallas as pl
from jax.experimental.pallas import tpu as pltpu
from jax.sharding import PartitionSpec as P


def grads_kernel(x_count, high_ref, own_ref, low_ref, in_ref, w_ref, dg_ref, wg_ref, s_ref):
    out_count, cells = own_ref.shape
    s_ref[:, :x_count] = jnp.zeros((3 * out_count, x_count), s_ref.dtype)
    s_ref[:, x_count + cells :] = jnp.zeros((3 * out_count, x_count), s_ref.dtype)
    column = lax.broadcasted_iota(jnp.int32, (out_count, cells), 1) % x_count
    for order, a in enumerate((1, 0, 2)):
        plane = (high_ref, own_ref, low_ref)[a][...]
        wide = plane.astype(jnp.float32)
        left = jnp.where(column == x_count - 1, 0.0, pltpu.roll(wide, cells - 1, 1))
        right = jnp.where(column == 0, 0.0, pltpu.roll(wide, 1, 1))
        for c, moved in enumerate((left, wide, right)):
            s_ref[c * out_count : (c + 1) * out_count, x_count : x_count + cells] = moved.astype(
                s_ref.dtype
            )
        for b in range(3):
            window = s_ref[:, (2 - b) * x_count : (2 - b) * x_count + cells]
            taps = jnp.concatenate([w_ref[9 * a + 3 * b + c] for c in range(3)], axis=1)
            term = jnp.dot(taps, window, preferred_element_type=jnp.float32)
            if order == 0 and b == 0:
                dg_ref[...] = term
            else:
                dg_ref[...] += term
            grad = lax.dot_general(
                in_ref[...], window, (((1,), (1,)), ((), ())), preferred_element_type=jnp.float32
            )
            for c in range(3):
                wg_ref[9 * a + 3 * b + c] = grad[:, c * out_count : (c + 1) * out_count]


def local(inputs, cotangent, weight):
    channels, rows, z_count, x_count = inputs.shape
    out_count = cotangent.shape[0]
    cells = rows * z_count * x_count
    count = lax.axis_size("gy")
    forward = [(i, i + 1) for i in range(count - 1)]
    backward = [(target, source) for source, target in forward]
    own = cotangent.reshape(out_count, cells)
    low = lax.ppermute(own, "gy", forward)
    high = lax.ppermute(own, "gy", backward)
    summed, taps = pl.pallas_call(
        functools.partial(grads_kernel, x_count),
        out_shape=(
            jax.ShapeDtypeStruct((channels, cells), jnp.float32),
            jax.ShapeDtypeStruct((27, channels, out_count), jnp.float32),
        ),
        in_specs=[pl.BlockSpec(memory_space=pltpu.VMEM)] * 5,
        out_specs=[pl.BlockSpec(memory_space=pltpu.VMEM)] * 2,
        scratch_shapes=[pltpu.VMEM((3 * out_count, cells + 2 * x_count), jnp.bfloat16)],
        compiler_params=pltpu.CompilerParams(vmem_limit_bytes=48 * 2**20),
        name="grads",
    )(high, own, low, inputs.reshape(channels, cells), weight)
    grad_rows = lax.psum_scatter(summed, "ch", scatter_dimension=0, tiled=True)
    input_grad = grad_rows.astype(jnp.bfloat16).reshape(-1, rows, z_count, x_count)
    norm_factor = 1.0 / math.sqrt(cells * count)
    weight_grad = lax.psum(taps, "gy") * norm_factor
    return (input_grad, weight_grad)


def solution(mesh):
    placed = (P(None, "gy", "grp", None), P("ch", "gy", "grp", None), P(None, None, "ch"))
    return jax.shard_map(
        local,
        mesh=mesh,
        in_specs=placed,
        out_specs=(P("ch", "gy", "grp", None), P("grp", None, "ch")),
        check_vma=False,
    )
```

```python
import functools
import math

import jax
import jax.numpy as jnp
from jax import lax
from jax.experimental import pallas as pl
from jax.experimental.pallas import tpu as pltpu
from jax.sharding import PartitionSpec as P

MESH = pl.DeviceIdType.MESH
SPAN = 166.0
PLANES = (1, 0, 2)
GROUPS = tuple((a, b) for a in PLANES for b in range(3))


def encode(values):
    top = jnp.max(jnp.abs(values), axis=0, keepdims=True)
    scale = (top * 1.01 + 1e-30).astype(jnp.bfloat16)
    size = jnp.exp(jnp.abs(values) * (SPAN / scale.astype(jnp.float32)) - SPAN / 2)
    code = jnp.where(values < 0, -size, size).astype(jnp.bfloat16)
    return code, jnp.broadcast_to(scale, (16, values.shape[1]))


def decode(code, scale):
    wide = code.astype(jnp.float32)
    step = scale.astype(jnp.float32)[0:1] * (1.0 / SPAN)
    size = (jnp.log(jnp.abs(wide)) + SPAN / 2) * step
    return jnp.where(wide < 0, -size, size)


def grads_kernel(
    x_count, count, norm, own_ref, in_ref, w_ref, out_ref, wg_ref,
    halo, s_ref, dg, dg_in, part, y_out, y_in, half, z_out, z_in, own_f, other_f,
    halo_s, halo_r, y_s, y_r, z_s, z_r, f_s, f_r, g_s, g_r, c_s, c_r,
):
    out_count, cells = own_ref.shape
    channels = in_ref.shape[0]
    me = lax.axis_index("gy")
    core = lax.axis_index("ch")
    parity = lax.rem(me, 2)
    place = lax.div(me, 2)
    partner = me + 1 - 2 * parity
    line = count // 2
    full = 3 * channels // 2
    per = z_out.shape[2] - 16

    def along(d):
        return 2 * lax.rem(place + d, line) + parity

    def copy(src, dst, send, recv, **where):
        return pltpu.make_async_remote_copy(
            src_ref=src, dst_ref=dst, send_sem=send, recv_sem=recv,
            device_id=where, device_id_type=MESH,
        )

    barrier = pltpu.get_barrier_semaphore()
    for d in range(1, count):
        pl.semaphore_signal(
            barrier, inc=1, device_id={"gy": lax.rem(me + d, count)}, device_id_type=MESH
        )
    pl.semaphore_signal(barrier, inc=1, device_id={"ch": 1 - core}, device_id_type=MESH)
    pl.semaphore_wait(barrier, count)

    down = copy(own_ref, halo.at[0], halo_s.at[0], halo_r.at[0], gy=jnp.maximum(me - 1, 0))
    up = copy(own_ref, halo.at[1], halo_s.at[1], halo_r.at[1], gy=jnp.minimum(me + 1, count - 1))

    @pl.when(me > 0)
    def _():
        down.start()

    @pl.when(me < count - 1)
    def _():
        up.start()

    @pl.when(me == 0)
    def _():
        halo[1] = jnp.zeros((out_count, cells), halo.dtype)

    @pl.when(me == count - 1)
    def _():
        halo[0] = jnp.zeros((out_count, cells), halo.dtype)

    y_copies = [
        copy(y_out.at[g], y_in.at[g], y_s.at[g], y_r.at[g], gy=partner) for g in range(9)
    ]
    z_copies = [
        [
            copy(z_out.at[g, d - 1], z_in.at[g, d - 1], z_s.at[g, d - 1], z_r.at[g, d - 1],
                 gy=along(d))
            for d in range(1, line)
        ]
        for g in range(9)
    ]
    f_copies = [
        [
            copy(own_f.at[g, place], own_f.at[g, place], f_s.at[g, d - 1], f_r.at[g, d - 1],
                 gy=along(d))
            for d in range(1, line)
        ]
        for g in range(9)
    ]
    g_copies = [
        copy(own_f.at[g], other_f.at[g], g_s.at[g], g_r.at[g], gy=partner) for g in range(9)
    ]

    def shift(a):
        if a == 0:
            plane = halo[0]
        elif a == 1:
            plane = own_ref[...]
        else:
            plane = halo[1]
        column = lax.broadcasted_iota(jnp.int32, (out_count, cells), 1) % x_count
        wide = plane.astype(jnp.float32)
        left = jnp.where(column == x_count - 1, 0.0, pltpu.roll(wide, cells - 1, 1))
        right = jnp.where(column == 0, 0.0, pltpu.roll(wide, 1, 1))
        edge = jnp.zeros((3 * out_count, x_count), s_ref.dtype)
        s_ref[a, :, :x_count] = edge
        s_ref[a, :, x_count + cells :] = edge
        for c, moved in enumerate((left, plane, right)):
            s_ref[a, c * out_count : (c + 1) * out_count, x_count : x_count + cells] = (
                moved.astype(s_ref.dtype)
            )

    def window(a, b):
        return s_ref[a, :, (2 - b) * x_count : (2 - b) * x_count + cells]

    def produce(g):
        grad = lax.dot_general(
            in_ref[...], window(*GROUPS[g]), (((1,), (1,)), ((), ())),
            preferred_element_type=jnp.float32,
        )
        for c in range(3):
            part[g, c * channels : (c + 1) * channels, :] = grad[
                :, c * out_count : (c + 1) * out_count
            ]
        code, scale = encode(part[g, pl.ds((1 - parity) * full, full), :])
        y_out[g, :full] = code
        y_out[g, full:] = scale
        y_copies[g].start()

    def spread(g):
        y_copies[g].wait_recv()
        half[g, :full] = part[g, pl.ds(parity * full, full), :] + decode(
            y_in[g, :full], y_in[g, full:]
        )
        if line * per > full:
            half[g, full:] = jnp.zeros((line * per - full, out_count), half.dtype)
        for d in range(1, line):
            target = lax.rem(place + d, line)
            code, scale = encode(half[g, pl.ds(target * per, per), :])
            z_out[g, d - 1, :per] = code
            z_out[g, d - 1, per:] = scale
            z_copies[g][d - 1].start()

    def collect(g):
        total = half[g, pl.ds(place * per, per), :]
        for d in range(1, line):
            z_copies[g][d - 1].wait_recv()
            total = total + decode(z_in[g, d - 1, :per], z_in[g, d - 1, per:])
        code, scale = encode(total * norm)
        own_f[g, place, :per] = code
        own_f[g, place, per:] = scale
        for d in range(1, line):
            f_copies[g][d - 1].start()

    def forward(g):
        for d in range(1, line):
            f_copies[g][d - 1].wait_recv()
        g_copies[g].start()

    def place_half(g, source, side):
        a, b = GROUPS[g]
        base = (9 * a + 3 * b) * channels
        for j in range(line):
            rows = min(per, full - j * per)
            if rows > 0:
                wg_ref[pl.ds(base + side * full + j * per, rows), :] = decode(
                    source[g, j, :rows], source[g, j, per:]
                )

    def finish(g):
        g_copies[g].wait_recv()
        place_half(g, other_f, 1 - parity)

    def dgrad(a):
        terms = None
        for b in range(3):
            taps = jnp.concatenate([w_ref[9 * a + 3 * b + c] for c in range(3)], axis=1)
            term = jnp.dot(taps, window(a, b), preferred_element_type=jnp.float32)
            terms = term if b == 0 else terms + term
        if a == PLANES[0]:
            dg[...] = terms
        else:
            dg[...] += terms

    owned = channels // 2
    shift(1)
    for g in range(3):
        produce(g)
    dgrad(1)

    @pl.when(me < count - 1)
    def _():
        down.wait_recv()

    shift(0)
    for g in range(3, 6):
        produce(g)
    for g in range(3):
        spread(g)

    @pl.when(me > 0)
    def _():
        up.wait_recv()

    shift(2)
    for g in range(6, 9):
        produce(g)
    for g in range(3):
        collect(g)
    dgrad(0)
    for g in range(3, 6):
        spread(g)
    for g in range(3):
        forward(g)
    dgrad(2)
    to_core = copy(dg.at[pl.ds((1 - core) * owned, owned)], dg_in, c_s, c_r, ch=1 - core)
    to_core.start()
    for g in range(3):
        spread(g + 6)
        collect(g + 3)
        place_half(g, own_f, parity)
    for g in range(3):
        collect(g + 6)
        forward(g + 3)
        finish(g)
        place_half(g + 3, own_f, parity)
    to_core.wait_recv()
    out_ref[...] = (dg[pl.ds(core * owned, owned), :] + dg_in[...]).astype(out_ref.dtype)
    for g in range(3):
        forward(g + 6)
        finish(g + 3)
        place_half(g + 6, own_f, parity)
    for g in range(6, 9):
        finish(g)

    @pl.when(me > 0)
    def _():
        down.wait_send()

    @pl.when(me < count - 1)
    def _():
        up.wait_send()

    to_core.wait_send()
    for g in range(9):
        y_copies[g].wait_send()
        g_copies[g].wait_send()
        for d in range(1, line):
            z_copies[g][d - 1].wait_send()
            f_copies[g][d - 1].wait_send()


def local(inputs, cotangent, weight):
    channels, rows, z_count, x_count = inputs.shape
    out_count = cotangent.shape[0]
    cells = rows * z_count * x_count
    count = lax.axis_size("gy")
    line = count // 2
    full = 3 * channels // 2
    per = -(-full // (line * 16)) * 16
    norm = 1.0 / math.sqrt(cells * count)
    bf16, f32 = jnp.bfloat16, jnp.float32
    dma = pltpu.SemaphoreType.DMA
    input_grad, weight_grad = pl.pallas_call(
        functools.partial(grads_kernel, x_count, count, norm),
        out_shape=(
            jax.ShapeDtypeStruct((channels // 2, cells), bf16),
            jax.ShapeDtypeStruct((27 * channels, out_count), f32),
        ),
        in_specs=[pl.BlockSpec(memory_space=pltpu.VMEM)] * 3,
        out_specs=[pl.BlockSpec(memory_space=pltpu.VMEM)] * 2,
        scratch_shapes=[
            pltpu.VMEM((2, out_count, cells), bf16),
            pltpu.VMEM((3, 3 * out_count, cells + 2 * x_count), bf16),
            pltpu.VMEM((channels, cells), f32),
            pltpu.VMEM((channels // 2, cells), f32),
            pltpu.VMEM((9, 3 * channels, out_count), f32),
            pltpu.VMEM((9, full + 16, out_count), bf16),
            pltpu.VMEM((9, full + 16, out_count), bf16),
            pltpu.VMEM((9, line * per, out_count), f32),
            pltpu.VMEM((9, line - 1, per + 16, out_count), bf16),
            pltpu.VMEM((9, line - 1, per + 16, out_count), bf16),
            pltpu.VMEM((9, line, per + 16, out_count), bf16),
            pltpu.VMEM((9, line, per + 16, out_count), bf16),
            dma((2,)),
            dma((2,)),
            dma((9,)),
            dma((9,)),
            dma((9, line - 1)),
            dma((9, line - 1)),
            dma((9, line - 1)),
            dma((9, line - 1)),
            dma((9,)),
            dma((9,)),
            dma(()),
            dma(()),
        ],
        compiler_params=pltpu.CompilerParams(
            collective_id=0, has_side_effects=True, vmem_limit_bytes=56 * 2**20
        ),
        name="grads",
    )(cotangent.reshape(out_count, cells), inputs.reshape(channels, cells), weight)
    return (
        input_grad.reshape(-1, rows, z_count, x_count),
        weight_grad.reshape(27, channels, out_count),
    )


def solution(mesh):
    placed = (P(None, "gy", "grp", None), P("ch", "gy", "grp", None), P(None, None, "ch"))
    return jax.shard_map(
        local,
        mesh=mesh,
        in_specs=placed,
        out_specs=(P("ch", "gy", "grp", None), P("grp", None, "ch")),
        check_vma=False,
    )
```

```python
import functools
import math

import jax
import jax.numpy as jnp
from jax import lax
from jax.experimental import pallas as pl
from jax.experimental.pallas import tpu as pltpu
from jax.sharding import PartitionSpec as P

MESH = pl.DeviceIdType.MESH
SPAN = 166.0
PLANES = (1, 0, 2)
GROUPS = tuple((a, b) for a in PLANES for b in range(3))


def encode(values):
    top = jnp.max(jnp.abs(values), axis=0, keepdims=True)
    scale = (top * 1.01 + 1e-30).astype(jnp.bfloat16)
    size = jnp.exp(jnp.abs(values) * (SPAN / scale.astype(jnp.float32)) - SPAN / 2)
    code = jnp.where(values < 0, -size, size).astype(jnp.bfloat16)
    return code, jnp.broadcast_to(scale, (16, values.shape[1]))


def decode(code, scale):
    wide = code.astype(jnp.float32)
    step = scale.astype(jnp.float32)[0:1] * (1.0 / SPAN)
    size = (jnp.log(jnp.abs(wide)) + SPAN / 2) * step
    return jnp.where(wide < 0, -size, size)


def grads_kernel(
    x_count, count, norm, own_ref, in_ref, w_ref, out_ref, wg_ref,
    halo, s_ref, dg, dg_in, part, y_out, y_in, half, zz_out, zz_in, z_out, z_in, done,
    halo_s, halo_r, y_s, y_r, z_s, z_r, f_s, f_r, g_s, g_r, c_s, c_r,
):
    out_count, cells = own_ref.shape
    channels = in_ref.shape[0]
    me = lax.axis_index("gy")
    core = lax.axis_index("ch")
    parity = lax.rem(me, 2)
    place = lax.div(me, 2)
    partner = me + 1 - 2 * parity
    line = count // 2
    full = 3 * channels // 2
    per = z_out.shape[2] - 16

    def along(d):
        return 2 * lax.rem(place + d, line) + parity

    def copy(src, dst, send, recv, **where):
        return pltpu.make_async_remote_copy(
            src_ref=src, dst_ref=dst, send_sem=send, recv_sem=recv,
            device_id=where, device_id_type=MESH,
        )

    barrier = pltpu.get_barrier_semaphore()
    for d in range(1, count):
        pl.semaphore_signal(
            barrier, inc=1, device_id={"gy": lax.rem(me + d, count)}, device_id_type=MESH
        )
    pl.semaphore_signal(barrier, inc=1, device_id={"ch": 1 - core}, device_id_type=MESH)
    pl.semaphore_wait(barrier, count)

    down = copy(own_ref, halo.at[0], halo_s.at[0], halo_r.at[0], gy=jnp.maximum(me - 1, 0))
    up = copy(own_ref, halo.at[1], halo_s.at[1], halo_r.at[1], gy=jnp.minimum(me + 1, count - 1))

    @pl.when(me > 0)
    def _():
        down.start()

    @pl.when(me == 0)
    def _():
        halo[1] = jnp.zeros((out_count, cells), halo.dtype)

    @pl.when(me == count - 1)
    def _():
        halo[0] = jnp.zeros((out_count, cells), halo.dtype)

    early = len(zz_out)
    lot = [slice(0, per + 16) if g < early else slice(None) for g in range(9)]
    y_copies = [
        copy(y_out.at[g, lot[g]], y_in.at[g, lot[g]], y_s.at[g], y_r.at[g], gy=partner)
        for g in range(9)
    ]
    z_copies = []
    f_copies = []
    for g in range(9):
        source, target = (zz_out, zz_in) if g < early else (z_out, z_in)
        slot = g if g < early else g - early
        z_copies.append([
            copy(source.at[slot, d - 1], target.at[slot, d - 1],
                 z_s.at[g, d - 1], z_r.at[g, d - 1], gy=along(d))
            for d in range(1, line)
        ])
        mine = done.at[g, parity, place]
        f_copies.append([
            copy(mine, mine, f_s.at[g, d - 1], f_r.at[g, d - 1], gy=along(d))
            for d in range(1, line)
        ])
    g_copies = [
        copy(done.at[g, parity], done.at[g, parity], g_s.at[g], g_r.at[g], gy=partner)
        for g in range(9)
    ]

    def shift(a):
        if a == 0:
            plane = halo[0]
        elif a == 1:
            plane = own_ref[...]
        else:
            plane = halo[1]
        column = lax.broadcasted_iota(jnp.int32, (out_count, cells), 1) % x_count
        wide = plane.astype(jnp.float32)
        left = jnp.where(column == x_count - 1, 0.0, pltpu.roll(wide, cells - 1, 1))
        right = jnp.where(column == 0, 0.0, pltpu.roll(wide, 1, 1))
        edge = jnp.zeros((3 * out_count, x_count), s_ref.dtype)
        s_ref[a, :, :x_count] = edge
        s_ref[a, :, x_count + cells :] = edge
        for c, moved in enumerate((left, plane, right)):
            s_ref[a, c * out_count : (c + 1) * out_count, x_count : x_count + cells] = (
                moved.astype(s_ref.dtype)
            )

    def window(a, b):
        return s_ref[a, :, (2 - b) * x_count : (2 - b) * x_count + cells]

    def produce(g):
        grad = lax.dot_general(
            in_ref[...], window(*GROUPS[g]), (((1,), (1,)), ((), ())),
            preferred_element_type=jnp.float32,
        )
        first, second, third = (
            grad[:, c * out_count : (c + 1) * out_count] for c in range(3)
        )
        middle = channels // 2
        part[g, 0, :channels] = first
        part[g, 0, channels:full] = second[:middle]
        part[g, 1, :middle] = second[middle:]
        part[g, 1, middle:full] = third
        if line * per > full:
            part[g, :, full:] = jnp.zeros((2, line * per - full, out_count), part.dtype)
        if g < early:
            for d in range(1, line):
                target = lax.rem(place + d, line)
                for side in range(2):
                    code, scale = encode(part[g, side, pl.ds(target * per, per), :])
                    zz_out[g, d - 1, side, :per] = code
                    zz_out[g, d - 1, side, per:] = scale
                z_copies[g][d - 1].start()
        else:
            code, scale = encode(part[g, 1 - parity, :full])
            y_out[g, :full] = code
            y_out[g, full:] = scale
            y_copies[g].start()

    def spread(g):
        if g < early:
            totals = [part[g, side, pl.ds(place * per, per), :] for side in (parity, 1 - parity)]
            for d in range(1, line):
                z_copies[g][d - 1].wait_recv()
                for n, side in enumerate((parity, 1 - parity)):
                    totals[n] += decode(
                        zz_in[g, d - 1, side, :per], zz_in[g, d - 1, side, per:]
                    )
            half[g, pl.ds(place * per, per), :] = totals[0]
            code, scale = encode(totals[1])
            y_out[g, :per] = code
            y_out[g, per : per + 16] = scale
            y_copies[g].start()
        else:
            y_copies[g].wait_recv()
            half[g, :full] = part[g, parity, :full] + decode(y_in[g, :full], y_in[g, full:])
            if line * per > full:
                half[g, full:] = jnp.zeros((line * per - full, out_count), half.dtype)
            for d in range(1, line):
                target = lax.rem(place + d, line)
                code, scale = encode(half[g, pl.ds(target * per, per), :])
                z_out[g - early, d - 1, :per] = code
                z_out[g - early, d - 1, per:] = scale
                z_copies[g][d - 1].start()

    def collect(g):
        total = half[g, pl.ds(place * per, per), :]
        if g < early:
            y_copies[g].wait_recv()
            total = total + decode(y_in[g, :per], y_in[g, per : per + 16])
        else:
            for d in range(1, line):
                z_copies[g][d - 1].wait_recv()
                total = total + decode(z_in[g - early, d - 1, :per], z_in[g - early, d - 1, per:])
        code, scale = encode(total * norm)
        done[g, parity, place, :per] = code
        done[g, parity, place, per:] = scale
        for d in range(1, line):
            f_copies[g][d - 1].start()

    def forward(g):
        for d in range(1, line):
            f_copies[g][d - 1].wait_recv()
        g_copies[g].start()

    def finish(g):
        a, b = GROUPS[g]
        g_copies[g].wait_recv()
        wg_ref[3 * a + b] = done[g]

    def dgrad(a):
        terms = None
        for b in range(3):
            taps = jnp.concatenate([w_ref[9 * a + 3 * b + c] for c in range(3)], axis=1)
            term = jnp.dot(taps, window(a, b), preferred_element_type=jnp.float32)
            terms = term if b == 0 else terms + term
        if a == PLANES[0]:
            dg[...] = terms
        else:
            dg[...] += terms

    owned = channels // 2
    shift(1)
    for g in range(3):
        produce(g)
    dgrad(1)

    @pl.when(me < count - 1)
    def _():
        up.start()
        down.wait_recv()

    shift(0)
    for g in range(3, 6):
        produce(g)
    for g in range(3):
        spread(g)
    dgrad(0)

    @pl.when(me > 0)
    def _():
        up.wait_recv()

    shift(2)
    for g in range(6, 9):
        produce(g)
    for g in range(3):
        collect(g)
        spread(g + 3)
    dgrad(2)
    to_core = copy(dg.at[pl.ds((1 - core) * owned, owned)], dg_in, c_s, c_r, ch=1 - core)
    to_core.start()
    for g in range(3):
        forward(g)
        collect(g + 3)
        spread(g + 6)
    for g in range(3):
        forward(g + 3)
        collect(g + 6)
    to_core.wait_recv()
    out_ref[...] = (dg[pl.ds(core * owned, owned), :] + dg_in[...]).astype(out_ref.dtype)
    for g in range(6):
        finish(g)
    for g in range(6, 9):
        forward(g)
    for g in range(6, 9):
        finish(g)

    @pl.when(me > 0)
    def _():
        down.wait_send()

    @pl.when(me < count - 1)
    def _():
        up.wait_send()

    to_core.wait_send()
    for g in range(9):
        y_copies[g].wait_send()
        g_copies[g].wait_send()
        for d in range(1, line):
            z_copies[g][d - 1].wait_send()
            f_copies[g][d - 1].wait_send()


def local(inputs, cotangent, weight):
    channels, rows, z_count, x_count = inputs.shape
    out_count = cotangent.shape[0]
    cells = rows * z_count * x_count
    count = lax.axis_size("gy")
    line = count // 2
    full = 3 * channels // 2
    per = -(-full // (line * 16)) * 16
    norm = 1.0 / math.sqrt(cells * count)
    bf16, f32 = jnp.bfloat16, jnp.float32
    dma = pltpu.SemaphoreType.DMA
    input_grad, codes = pl.pallas_call(
        functools.partial(grads_kernel, x_count, count, norm),
        out_shape=(
            jax.ShapeDtypeStruct((channels // 2, cells), bf16),
            jax.ShapeDtypeStruct((9, 2, line, per + 16, out_count), bf16),
        ),
        in_specs=[pl.BlockSpec(memory_space=pltpu.VMEM)] * 3,
        out_specs=[pl.BlockSpec(memory_space=pltpu.VMEM)] * 2,
        scratch_shapes=[
            pltpu.VMEM((2, out_count, cells), bf16),
            pltpu.VMEM((3, 3 * out_count, cells + 2 * x_count), bf16),
            pltpu.VMEM((channels, cells), f32),
            pltpu.VMEM((channels // 2, cells), f32),
            pltpu.VMEM((9, 2, line * per, out_count), f32),
            pltpu.VMEM((9, full + 16, out_count), bf16),
            pltpu.VMEM((9, full + 16, out_count), bf16),
            pltpu.VMEM((9, line * per, out_count), f32),
            pltpu.VMEM((3, line - 1, 2, per + 16, out_count), bf16),
            pltpu.VMEM((3, line - 1, 2, per + 16, out_count), bf16),
            pltpu.VMEM((6, line - 1, per + 16, out_count), bf16),
            pltpu.VMEM((6, line - 1, per + 16, out_count), bf16),
            pltpu.VMEM((9, 2, line, per + 16, out_count), bf16),
            dma((2,)),
            dma((2,)),
            dma((9,)),
            dma((9,)),
            dma((9, line - 1)),
            dma((9, line - 1)),
            dma((9, line - 1)),
            dma((9, line - 1)),
            dma((9,)),
            dma((9,)),
            dma(()),
            dma(()),
        ],
        compiler_params=pltpu.CompilerParams(
            collective_id=0, has_side_effects=True, vmem_limit_bytes=56 * 2**20
        ),
        name="grads",
    )(cotangent.reshape(out_count, cells), inputs.reshape(channels, cells), weight)
    wide = codes[..., :per, :].astype(f32)
    step = codes[..., per : per + 1, :].astype(f32) * (1.0 / SPAN)
    size = (jnp.log(jnp.abs(wide)) + SPAN / 2) * step
    weight_grad = jnp.where(wide < 0, -size, size).reshape(9, 2, line * per, out_count)[:, :, :full]
    return (
        input_grad.reshape(-1, rows, z_count, x_count),
        weight_grad.reshape(27, channels, out_count),
    )


def solution(mesh):
    placed = (P(None, "gy", "grp", None), P("ch", "gy", "grp", None), P(None, None, "ch"))
    return jax.shard_map(
        local,
        mesh=mesh,
        in_specs=placed,
        out_specs=(P("ch", "gy", "grp", None), P("grp", None, "ch")),
        check_vma=False,
    )
```

```python
import functools
import math

import jax
import jax.numpy as jnp
from jax import lax
from jax.experimental import pallas as pl
from jax.experimental.pallas import tpu as pltpu
from jax.sharding import PartitionSpec as P

MESH = pl.DeviceIdType.MESH
SPAN = 166.0
PLANES = (1, 0, 2)
GROUPS = tuple((a, b) for a in PLANES for b in range(3))


def encode(values):
    top = jnp.max(jnp.abs(values), axis=0, keepdims=True)
    scale = (top * 1.01 + 1e-30).astype(jnp.bfloat16)
    size = jnp.exp(jnp.abs(values) * (SPAN / scale.astype(jnp.float32)) - SPAN / 2)
    code = jnp.where(values < 0, -size, size).astype(jnp.bfloat16)
    return code, jnp.broadcast_to(scale, (16, values.shape[1]))


def decode(code, scale):
    wide = code.astype(jnp.float32)
    step = scale.astype(jnp.float32)[0:1] * (1.0 / SPAN)
    size = (jnp.log(jnp.abs(wide)) + SPAN / 2) * step
    return jnp.where(wide < 0, -size, size)


def grads_kernel(
    x_count, count, norm, own_ref, in_ref, w_ref, out_ref, wg_ref,
    halo, s_ref, dg, dg_in, part, y_out, y_in, half, zz_out, zz_in, z_out, z_in, done,
    wide_ref, flat_in,
    halo_s, halo_r, y_s, y_r, z_s, z_r, f_s, f_r, g_s, g_r, c_s, c_r,
):
    out_count, z_count, _ = own_ref.shape
    cells = z_count * x_count
    channels = in_ref.shape[0]
    me = lax.axis_index("gy")
    core = lax.axis_index("ch")
    parity = lax.rem(me, 2)
    place = lax.div(me, 2)
    partner = me + 1 - 2 * parity
    line = count // 2
    full = 3 * channels // 2
    per = z_out.shape[2] - 16

    def along(d):
        return 2 * lax.rem(place + d, line) + parity

    def copy(src, dst, send, recv, **where):
        return pltpu.make_async_remote_copy(
            src_ref=src, dst_ref=dst, send_sem=send, recv_sem=recv,
            device_id=where, device_id_type=MESH,
        )

    barrier = pltpu.get_barrier_semaphore()
    for d in range(1, count):
        pl.semaphore_signal(
            barrier, inc=1, device_id={"gy": lax.rem(me + d, count)}, device_id_type=MESH
        )
    pl.semaphore_signal(barrier, inc=1, device_id={"ch": 1 - core}, device_id_type=MESH)
    pl.semaphore_wait(barrier, count)

    down = copy(own_ref, halo.at[0], halo_s.at[0], halo_r.at[0], gy=jnp.maximum(me - 1, 0))
    up = copy(own_ref, halo.at[1], halo_s.at[1], halo_r.at[1], gy=jnp.minimum(me + 1, count - 1))

    @pl.when(me > 0)
    def _():
        down.start()

    @pl.when(me == 0)
    def _():
        halo[1] = jnp.zeros(own_ref.shape, halo.dtype)

    @pl.when(me == count - 1)
    def _():
        halo[0] = jnp.zeros(own_ref.shape, halo.dtype)

    early = len(zz_out)
    lot = [slice(0, per + 16) if g < early else slice(None) for g in range(9)]
    y_copies = [
        copy(y_out.at[g, lot[g]], y_in.at[g, lot[g]], y_s.at[g], y_r.at[g], gy=partner)
        for g in range(9)
    ]
    z_copies = []
    f_copies = []
    for g in range(9):
        source, target = (zz_out, zz_in) if g < early else (z_out, z_in)
        slot = g if g < early else g - early
        z_copies.append([
            copy(source.at[slot, d - 1], target.at[slot, d - 1],
                 z_s.at[g, d - 1], z_r.at[g, d - 1], gy=along(d))
            for d in range(1, line)
        ])
        mine = done.at[g, parity, place]
        f_copies.append([
            copy(mine, mine, f_s.at[g, d - 1], f_r.at[g, d - 1], gy=along(d))
            for d in range(1, line)
        ])
    g_copies = [
        copy(done.at[g, parity], done.at[g, parity], g_s.at[g], g_r.at[g], gy=partner)
        for g in range(9)
    ]

    def flatten(value):
        rows = value.shape[0]
        wide_ref[:rows] = value.astype(jnp.float32)
        return jnp.concatenate([wide_ref[:rows, z, :] for z in range(z_count)], axis=1)

    def shift(a):
        if a == 0:
            plane = halo[0]
        elif a == 1:
            plane = own_ref[...]
        else:
            plane = halo[1]
        column = lax.broadcasted_iota(jnp.int32, (out_count, cells), 1) % x_count
        wide = flatten(plane)
        left = jnp.where(column == x_count - 1, 0.0, pltpu.roll(wide, cells - 1, 1))
        right = jnp.where(column == 0, 0.0, pltpu.roll(wide, 1, 1))
        edge = jnp.zeros((3 * out_count, x_count), s_ref.dtype)
        s_ref[a, :, :x_count] = edge
        s_ref[a, :, x_count + cells :] = edge
        for c, moved in enumerate((left, wide, right)):
            s_ref[a, c * out_count : (c + 1) * out_count, x_count : x_count + cells] = (
                moved.astype(s_ref.dtype)
            )

    def window(a, b):
        return s_ref[a, :, (2 - b) * x_count : (2 - b) * x_count + cells]

    def produce(g):
        grad = lax.dot_general(
            flat_in[...], window(*GROUPS[g]), (((1,), (1,)), ((), ())),
            preferred_element_type=jnp.float32,
        )
        first, second, third = (
            grad[:, c * out_count : (c + 1) * out_count] for c in range(3)
        )
        middle = channels // 2
        part[g, 0, :channels] = first
        part[g, 0, channels:full] = second[:middle]
        part[g, 1, :middle] = second[middle:]
        part[g, 1, middle:full] = third
        if line * per > full:
            part[g, :, full:] = jnp.zeros((2, line * per - full, out_count), part.dtype)
        if g < early:
            for d in range(1, line):
                target = lax.rem(place + d, line)
                for side in range(2):
                    code, scale = encode(part[g, side, pl.ds(target * per, per), :])
                    zz_out[g, d - 1, side, :per] = code
                    zz_out[g, d - 1, side, per:] = scale
                z_copies[g][d - 1].start()
        else:
            code, scale = encode(part[g, 1 - parity, :full])
            y_out[g, :full] = code
            y_out[g, full:] = scale
            y_copies[g].start()

    def spread(g):
        if g < early:
            totals = [part[g, side, pl.ds(place * per, per), :] for side in (parity, 1 - parity)]
            for d in range(1, line):
                z_copies[g][d - 1].wait_recv()
                for n, side in enumerate((parity, 1 - parity)):
                    totals[n] += decode(
                        zz_in[g, d - 1, side, :per], zz_in[g, d - 1, side, per:]
                    )
            half[g, pl.ds(place * per, per), :] = totals[0]
            code, scale = encode(totals[1])
            y_out[g, :per] = code
            y_out[g, per : per + 16] = scale
            y_copies[g].start()
        else:
            y_copies[g].wait_recv()
            half[g, :full] = part[g, parity, :full] + decode(y_in[g, :full], y_in[g, full:])
            if line * per > full:
                half[g, full:] = jnp.zeros((line * per - full, out_count), half.dtype)
            for d in range(1, line):
                target = lax.rem(place + d, line)
                code, scale = encode(half[g, pl.ds(target * per, per), :])
                z_out[g - early, d - 1, :per] = code
                z_out[g - early, d - 1, per:] = scale
                z_copies[g][d - 1].start()

    def collect(g):
        total = half[g, pl.ds(place * per, per), :]
        if g < early:
            y_copies[g].wait_recv()
            total = total + decode(y_in[g, :per], y_in[g, per : per + 16])
        else:
            for d in range(1, line):
                z_copies[g][d - 1].wait_recv()
                total = total + decode(z_in[g - early, d - 1, :per], z_in[g - early, d - 1, per:])
        code, scale = encode(total * norm)
        done[g, parity, place, :per] = code
        done[g, parity, place, per:] = scale
        for d in range(1, line):
            f_copies[g][d - 1].start()

    def forward(g):
        for d in range(1, line):
            f_copies[g][d - 1].wait_recv()
        g_copies[g].start()

    def finish(g):
        a, b = GROUPS[g]
        g_copies[g].wait_recv()
        wg_ref[3 * a + b] = done[g]

    def dgrad(a):
        terms = None
        for b in range(3):
            taps = jnp.concatenate([w_ref[9 * a + 3 * b + c] for c in range(3)], axis=1)
            term = jnp.dot(taps, window(a, b), preferred_element_type=jnp.float32)
            terms = term if b == 0 else terms + term
        if a == PLANES[0]:
            dg[...] = terms
        else:
            dg[...] += terms

    owned = channels // 2
    flat_in[...] = flatten(in_ref[...]).astype(flat_in.dtype)
    shift(1)
    for g in range(3):
        produce(g)
    dgrad(1)

    @pl.when(me < count - 1)
    def _():
        up.start()
        down.wait_recv()

    shift(0)
    for g in range(3, 6):
        produce(g)
    for g in range(3):
        spread(g)
    dgrad(0)

    @pl.when(me > 0)
    def _():
        up.wait_recv()

    shift(2)
    for g in range(6, 9):
        produce(g)
    for g in range(3):
        collect(g)
        spread(g + 3)
    dgrad(2)
    to_core = copy(dg.at[pl.ds((1 - core) * owned, owned)], dg_in, c_s, c_r, ch=1 - core)
    to_core.start()
    for g in range(3):
        forward(g)
        collect(g + 3)
        spread(g + 6)
    for g in range(3):
        forward(g + 3)
        collect(g + 6)
    to_core.wait_recv()
    final = dg[pl.ds(core * owned, owned), :] + dg_in[...]
    for z in range(z_count):
        wide_ref[:owned, z, :] = final[:, z * x_count : (z + 1) * x_count]
    out_ref[...] = wide_ref[:owned].astype(out_ref.dtype)
    for g in range(6):
        finish(g)
    for g in range(6, 9):
        forward(g)
    for g in range(6, 9):
        finish(g)

    @pl.when(me > 0)
    def _():
        down.wait_send()

    @pl.when(me < count - 1)
    def _():
        up.wait_send()

    to_core.wait_send()
    for g in range(9):
        y_copies[g].wait_send()
        g_copies[g].wait_send()
        for d in range(1, line):
            z_copies[g][d - 1].wait_send()
            f_copies[g][d - 1].wait_send()


def local(inputs, cotangent, weight):
    channels, rows, z_count, x_count = inputs.shape
    out_count = cotangent.shape[0]
    cells = rows * z_count * x_count
    count = lax.axis_size("gy")
    line = count // 2
    full = 3 * channels // 2
    per = -(-full // (line * 16)) * 16
    norm = 1.0 / math.sqrt(cells * count)
    bf16, f32 = jnp.bfloat16, jnp.float32
    dma = pltpu.SemaphoreType.DMA
    input_grad, codes = pl.pallas_call(
        functools.partial(grads_kernel, x_count, count, norm),
        out_shape=(
            jax.ShapeDtypeStruct((channels // 2, rows * z_count, x_count), bf16),
            jax.ShapeDtypeStruct((9, 2, line, per + 16, out_count), bf16),
        ),
        in_specs=[pl.BlockSpec(memory_space=pltpu.VMEM)] * 3,
        out_specs=[pl.BlockSpec(memory_space=pltpu.VMEM)] * 2,
        scratch_shapes=[
            pltpu.VMEM((2, out_count, rows * z_count, x_count), bf16),
            pltpu.VMEM((3, 3 * out_count, cells + 2 * x_count), bf16),
            pltpu.VMEM((channels, cells), f32),
            pltpu.VMEM((channels // 2, cells), f32),
            pltpu.VMEM((9, 2, line * per, out_count), f32),
            pltpu.VMEM((9, full + 16, out_count), bf16),
            pltpu.VMEM((9, full + 16, out_count), bf16),
            pltpu.VMEM((9, line * per, out_count), f32),
            pltpu.VMEM((3, line - 1, 2, per + 16, out_count), bf16),
            pltpu.VMEM((3, line - 1, 2, per + 16, out_count), bf16),
            pltpu.VMEM((6, line - 1, per + 16, out_count), bf16),
            pltpu.VMEM((6, line - 1, per + 16, out_count), bf16),
            pltpu.VMEM((9, 2, line, per + 16, out_count), bf16),
            pltpu.VMEM((channels, rows * z_count, x_count), f32),
            pltpu.VMEM((channels, cells), bf16),
            dma((2,)),
            dma((2,)),
            dma((9,)),
            dma((9,)),
            dma((9, line - 1)),
            dma((9, line - 1)),
            dma((9, line - 1)),
            dma((9, line - 1)),
            dma((9,)),
            dma((9,)),
            dma(()),
            dma(()),
        ],
        compiler_params=pltpu.CompilerParams(
            collective_id=0, has_side_effects=True, vmem_limit_bytes=56 * 2**20
        ),
        name="grads",
    )(
        cotangent.reshape(out_count, rows * z_count, x_count),
        inputs.reshape(channels, rows * z_count, x_count),
        weight,
    )
    wide = codes[..., :per, :].astype(f32)
    step = codes[..., per : per + 1, :].astype(f32) * (1.0 / SPAN)
    size = (jnp.log(jnp.abs(wide)) + SPAN / 2) * step
    weight_grad = jnp.where(wide < 0, -size, size).reshape(9, 2, line * per, out_count)[:, :, :full]
    return (
        input_grad.reshape(-1, rows, z_count, x_count),
        weight_grad.reshape(27, channels, out_count),
    )


def solution(mesh):
    placed = (P(None, "gy", "grp", None), P("ch", "gy", "grp", None), P(None, None, "ch"))
    return jax.shard_map(
        local,
        mesh=mesh,
        in_specs=placed,
        out_specs=(P("ch", "gy", "grp", None), P("grp", None, "ch")),
        check_vma=False,
    )
```
